32 devices in a mesh: ctx: 16 (over z, y, x), tp: 2 (over core).
Axes of the slice: x: 2, y: 2, z: 4, core: 2. Of those that a mesh axis runs over, the one named last changes fastest.
Arguments:
- gate_out: bfloat16 [8192, 4096], P('ctx', 'tp'), may hold values from -6 to 6
- gate_in: bfloat16 [8192, 4096], P('ctx', 'tp'), may hold values from -6 to 6
- signal: bfloat16 [8192, 4096], P('ctx', 'tp'), may hold values from -6 to 6
- decay_rates: float32 [16, 4096], P(None, 'tp'), may hold values from 3.90625e-06 to 0.1, as said below
- residues: float32 [16, 4096], P(None, 'tp'), may hold values from -0.6 to 0.6
- skip_gain: float32 [4096], P('tp'), may hold values from -4 to 4
- out_proj: bfloat16 [4096, 4096], P('tp'), may hold values from -0.09375 to 0.09375
- doc_lengths: int32 [8], replicated, may hold values from 1 to 5120, 8192 in all
Outputs:
- layer_out: bfloat16 [8192, 4096], P(('ctx', 'tp'))
The draws below stay inside these ranges and needn't reach their ends.
Inputs may be any that keep to these rules, and one draw needn't show every extreme that they name: `doc_lengths`: 8 documents laid end to end, lengths summing to 8192. `decay_rates`: positive.
All inputs are finite; a program needn't handle non-finite values.
Results may differ from the reference program's by a relative error of at most 0.017.
Values may be sent and summed in bfloat16 or wider, within the bound.
A program may use at most 128 MiB of HBM per device.

```python
import math
import jax
import jax.numpy as jnp
import numpy as np
from jax import lax

C_WIN = 4096
OUTW = 4096
R_MODES = 16
TOKENS = 8192
NDOCS = 8
DOC_MOST = 5120
N_TP = 2


def mode_law(key):
    shape_modes = (R_MODES, C_WIN)
    slow_share = 0.5
    is_slow = jax.random.uniform(jax.random.fold_in(key, 11), shape_modes, jnp.float32) < slow_share
    slow_rate = jnp.exp(jax.random.uniform(jax.random.fold_in(key, 12), shape_modes, jnp.float32, minval=math.log(0.02 / DOC_MOST), maxval=math.log(2.0 / DOC_MOST)))
    fast_rate = jnp.exp(jax.random.uniform(jax.random.fold_in(key, 13), shape_modes, jnp.float32, minval=math.log(0.02), maxval=math.log(0.1)))
    rates = jnp.where(is_slow, slow_rate, fast_rate)
    spread = jnp.where(is_slow, 0.3 / math.sqrt(DOC_MOST), 0.15)
    return (rates, spread)


def draw_decay_rates(key, part):
    rates, spread = mode_law(key)
    return rates.astype(jnp.float32)


def draw_residues(key, part):
    rates, spread = mode_law(key)
    normal_vals = jnp.clip(jax.random.normal(jax.random.fold_in(key, 14), (R_MODES, C_WIN), jnp.float32), -4.0, 4.0)
    return (spread * normal_vals).astype(jnp.float32)


def block_scale(stream_key, extent, pieces, smallest, largest):
    factor_of, own = 1.0, jax.random.fold_in(stream_key, 6)
    for axis_at, parts in pieces:
        draws = jnp.exp(jax.random.uniform(jax.random.fold_in(own, axis_at), (parts,), jnp.float32, smallest / len(pieces), largest / len(pieces)))
        factor_of = factor_of * jnp.repeat(draws, extent[axis_at] // parts).reshape([-1 if axis == axis_at else 1 for axis in range(len(extent))])
    return factor_of


def split_up(amount, total, bound, lean):
    loads = [(1 << 20) // math.isqrt(grade ** lean) + 1 for grade in range(2, amount + 1)]
    rest, holding = total - bound - (amount - 1), [1] * (amount - 1)
    while rest > 0:
        candidates = [i for i in range(amount - 1) if holding[i] < bound]
        mass, remaining = sum([loads[i] for i in candidates]), rest
        for i in candidates:
            extra = min(bound - holding[i], max(1, remaining * loads[i] // mass), rest)
            holding[i] = holding[i] + extra
            rest = rest - extra
    return np.array([bound] + holding)


def uneven_parts(own_key, number_of, total, reach, slope):
    if number_of == 2:
        one = jax.random.randint(own_key, (), max(1, total - reach), min(reach, total - 1) + 1)
        return jnp.stack([one, total - one])
    tallies = jnp.asarray(split_up(number_of, total, reach, slope), jnp.int32)
    couples = (number_of - 1) // 2
    giver, receiver = tallies[1:1 + 2 * couples:2], tallies[2:2 + 2 * couples:2]
    slack = jnp.minimum(giver - 1, reach - receiver)
    moved = jax.random.randint(jax.random.fold_in(own_key, 1), (couples,), 0, 1 << 20) % (slack + 1)
    tallies = tallies.at[1:1 + 2 * couples:2].set(giver - moved).at[2:2 + 2 * couples:2].set(receiver + moved)
    return tallies[jax.random.permutation(jax.random.fold_in(own_key, 2), number_of)]


def bell_draw(own_key, dims, width, reach, pieces=(), held_as=jnp.bfloat16):
    gain = block_scale(own_key, dims, pieces, -0.22, 0.18) if pieces else 1.0
    array = jax.random.normal(own_key, dims, jnp.float32) * width * gain
    return jnp.minimum(jnp.maximum(array, -reach), reach).astype(held_as)


def setup_inputs(seed: int = 0) -> dict:
    seeds = jax.random.split(jax.random.key(seed), 9)
    return {
        "gate_out": bell_draw(seeds[0], (TOKENS, C_WIN), 1.0, 6.0, ((0, 16), (1, 2))),
        "gate_in": bell_draw(seeds[1], (TOKENS, C_WIN), 1.0, 6.0, ((0, 16), (1, 2))),
        "signal": bell_draw(seeds[2], (TOKENS, C_WIN), 1.0, 6.0, ((0, 16), (1, 2))),
        "decay_rates": draw_decay_rates(jax.random.fold_in(seeds[8], 71), 0),
        "residues": draw_residues(jax.random.fold_in(seeds[8], 71), 0),
        "skip_gain": bell_draw(seeds[5], (C_WIN,), 1.0, 4.0, ((0, 2),), jnp.float32),
        "out_proj": bell_draw(seeds[6], (C_WIN, OUTW), C_WIN ** -0.5, 0.09375, ((0, 2),)),
        "doc_lengths": uneven_parts(seeds[7], NDOCS, TOKENS, DOC_MOST, 1).astype(jnp.int32),
    }


def reference(gate_out, gate_in, signal, decay_rates, residues, skip_gain, out_proj, doc_lengths):
    feed_in = gate_in.astype(jnp.float32) * signal.astype(jnp.float32)
    doc_ends = jnp.cumsum(doc_lengths).astype(jnp.int32)
    doc_starts = (doc_ends - doc_lengths).astype(jnp.int32)
    start_flags = jnp.zeros((TOKENS,), jnp.float32).at[doc_starts].set(1.0)
    keep_flags = 1.0 - start_flags
    decay = jnp.exp(-decay_rates)

    def advance(carry_state, inputs):
        token_row, keep_mask = inputs
        carry_state = decay * carry_state * keep_mask + token_row[None, :]
        return carry_state, jnp.sum(residues * carry_state, axis=0)

    zero_state = jnp.zeros((R_MODES, C_WIN), jnp.float32)
    _, conv_out = lax.scan(advance, zero_state, (feed_in, keep_flags))
    mixed = conv_out + skip_gain[None, :] * feed_in
    hidden = (gate_out.astype(jnp.float32) * mixed).astype(jnp.bfloat16)
    group_width = C_WIN // N_TP
    summed = jnp.zeros((TOKENS, OUTW), jnp.float32)
    for group_idx in range(N_TP):
        lower = group_idx * group_width
        partial_sum = jnp.dot(hidden[:, lower:lower + group_width].astype(jnp.float32),
                              out_proj[lower:lower + group_width, :].astype(jnp.float32),
                              precision=lax.Precision.HIGHEST)
        rounded = lax.optimization_barrier(partial_sum.astype(jnp.bfloat16))
        summed = summed + rounded.astype(jnp.float32)
    return summed.astype(jnp.bfloat16)
```

```python
import functools

import jax
import jax.numpy as jnp
from jax import lax
from jax.experimental import pallas as pl
from jax.experimental.pallas import tpu as pltpu
from jax.sharding import PartitionSpec as P

LANES = 128
SUB = 8
STEP = 8
CHUNK = 64


def spread(x_ref, gate_ref, sig_ref, q, q8, keep=None):
    rows = gate_ref.shape[0]

    def tile(i, _):
        t0 = pl.multiple_of(i * 16, 16)
        for j in range(q):
            cols = pl.ds(j * LANES, LANES)
            x = gate_ref[pl.ds(t0, 16), cols].astype(jnp.float32) * sig_ref[
                pl.ds(t0, 16), cols
            ].astype(jnp.float32)
            if keep is not None:
                x = x * keep(t0)
            x_ref[pl.ds(t0 * q8 + j, 16, stride=q8), :] = x
        return 0

    lax.fori_loop(0, rows // 16, tile, 0)


def end_state_kernel(modes, q, q8, last_ref, gate_ref, sig_ref, decay_ref, end_ref, x_ref, s_ref):
    step = pl.program_id(0)
    rows = gate_ref.shape[0]

    @pl.when(step == 0)
    def _():
        s_ref[...] = jnp.zeros_like(s_ref)

    last = last_ref[0]
    base = step * rows

    def keep(t0):
        at = base + t0 + lax.broadcasted_iota(jnp.int32, (16, LANES), 0)
        return (at >= last).astype(jnp.float32)

    @pl.when(base + rows > last)
    def _():
        spread(x_ref, gate_ref, sig_ref, q, q8, keep)
        for h in range(0, q8, SUB):
            d = [decay_ref[n, pl.ds(h, SUB), :] for n in range(modes)]

            def block(i, s):
                s = list(s)
                for k in range(STEP):
                    at = pl.multiple_of((i * STEP + k) * q8 + h, SUB)
                    x = x_ref[pl.ds(at, SUB), :]
                    for n in range(modes):
                        s[n] = d[n] * s[n] + x
                return tuple(s)

            out = lax.fori_loop(
                0, rows // STEP, block, tuple(s_ref[n, pl.ds(h, SUB), :] for n in range(modes))
            )
            for n in range(modes):
                s_ref[n, pl.ds(h, SUB), :] = out[n]

    @pl.when(step == pl.num_programs(0) - 1)
    def _():
        end_ref[...] = s_ref[...].astype(end_ref.dtype)


def exchange_kernel(n, length, plan, end_ref, rate_ref, mask_ref, out_ref, send_buf, slots, send_sem, recv_sem):
    me = lax.axis_index("ctx")
    offsets = sorted({off for stage in plan for off, _ in stage})
    barrier = pltpu.get_barrier_semaphore()
    for off in offsets:

        @pl.when(me >= off)
        def _():
            pl.semaphore_signal(
                barrier, inc=1, device_id={"ctx": me - off}, device_id_type=pl.DeviceIdType.MESH
            )

    peers = sum((me + off < n).astype(jnp.int32) for off in offsets)

    @pl.when(me + 1 < n)
    def _():
        pl.semaphore_wait(barrier, peers)

    def copy(k, stage, off):
        src = end_ref if stage == 0 else send_buf.at[stage - 1]
        return pltpu.make_async_remote_copy(
            src_ref=src,
            dst_ref=slots.at[k],
            send_sem=send_sem.at[k],
            recv_sem=recv_sem.at[k],
            device_id={"ctx": jnp.minimum(me + off, n - 1)},
            device_id_type=pl.DeviceIdType.MESH,
        )

    out_ref[...] = jnp.zeros_like(out_ref)
    k0 = 0
    for stage, hops in enumerate(plan):
        if stage:
            send_buf[stage - 1] = out_ref[...].astype(send_buf.dtype)
        for k, (off, gap) in enumerate(hops, k0):

            @pl.when(me + off < n)
            def _():
                copy(k, stage, off).start()

        for k, (off, gap) in enumerate(hops, k0):

            @pl.when(me >= off)
            def _():
                weight = jnp.exp(rate_ref[...] * (-float(length * gap))) * mask_ref[pl.ds(k, 1), :]
                copy(k, stage, off).wait_recv()
                out_ref[...] += weight * slots[k].astype(jnp.float32)

        k0 += len(hops)
    k = 0
    for stage, hops in enumerate(plan):
        for off, gap in hops:

            @pl.when(me + off < n)
            def _():
                copy(k, stage, off).wait_send()

            k += 1


def conv_kernel(
    modes, q, q8, keep_ref, cut_ref, go_ref, gate_ref, sig_ref, decay_ref, res_ref, skip_ref,
    carried_ref, hidden_ref, x_ref, y_ref, s_ref,
):
    step = pl.program_id(0)
    rows = gate_ref.shape[0]

    @pl.when(step == 0)
    def _():
        s_ref[...] = carried_ref[...]

    spread(x_ref, gate_ref, sig_ref, q, q8)
    for h in range(0, q8, SUB):
        d = [decay_ref[n, pl.ds(h, SUB), :] for n in range(modes)]
        r = [res_ref[n, pl.ds(h, SUB), :] for n in range(modes)]
        skip = skip_ref[pl.ds(h, SUB), :]

        def run(i, s, cut):
            s = list(s)
            for k in range(STEP):
                at = pl.multiple_of((i * STEP + k) * q8 + h, SUB)
                x = x_ref[pl.ds(at, SUB), :]
                parts = [skip * x, None, None, None]
                if cut:
                    keep = keep_ref[step * rows + i * STEP + k]
                for n in range(modes):
                    old = s[n] * keep if cut else s[n]
                    s[n] = d[n] * old + x
                    term = r[n] * s[n]
                    p = parts[n % 4]
                    parts[n % 4] = term if p is None else p + term
                y_ref[pl.ds(at, SUB), :] = (parts[0] + parts[1]) + (parts[2] + parts[3])
            return tuple(s)

        def block(i, s):
            return lax.cond(
                cut_ref[step * (rows // STEP) + i] > 0,
                lambda s: run(i, s, True),
                lambda s: run(i, s, False),
                s,
            )

        out = lax.fori_loop(
            0, rows // STEP, block, tuple(s_ref[n, pl.ds(h, SUB), :] for n in range(modes))
        )
        for n in range(modes):
            s_ref[n, pl.ds(h, SUB), :] = out[n]

    def tile(i, _):
        t0 = pl.multiple_of(i * 16, 16)
        for j in range(q):
            cols = pl.ds(j * LANES, LANES)
            y = y_ref[pl.ds(t0 * q8 + j, 16, stride=q8), :]
            g = go_ref[pl.ds(t0, 16), cols].astype(jnp.float32)
            hidden_ref[pl.ds(t0, 16), cols] = (g * y).astype(hidden_ref.dtype)
        return 0

    lax.fori_loop(0, rows // 16, tile, 0)


def scan_plan(n):
    plan = [[(off, off - 1) for off in range(1, min(4, n - 1) + 1)]]
    unit = 4
    while unit < n:
        plan.append([(off, off) for off in (unit, 2 * unit, 3 * unit) if off < n])
        unit *= 4
    return plan


def make(n, tp):
    plan = scan_plan(n)
    hops = sum(len(stage) for stage in plan)

    def per_device(gate_out, gate_in, signal, decay_rates, residues, skip_gain, out_proj, doc_lengths):
        length, channels = signal.shape
        modes = decay_rates.shape[0]
        q = channels // LANES
        q8 = -(-q // SUB) * SUB
        chunk = min(CHUNK, length)
        me = lax.axis_index("ctx")
        begin = me * length
        doc_starts = jnp.cumsum(doc_lengths) - doc_lengths
        local = doc_starts - begin
        inside = (local >= 0) & (local < length)
        last = jnp.max(jnp.where(inside, local, 0)).astype(jnp.int32).reshape(1)
        at = jnp.arange(length, dtype=jnp.int32)
        opening = jnp.any(local[None, :] == at[:, None], axis=1)
        keep = 1.0 - opening.astype(jnp.float32)
        cut = jnp.max(opening.reshape(length // STEP, STEP).astype(jnp.int32), axis=1)
        head = jnp.max(jnp.where(doc_starts <= begin, doc_starts, 0))
        ids = jnp.array([gap for stage in plan for _, gap in stage], jnp.int32)
        mask = (head < (me - ids) * length).astype(jnp.float32)
        mask = jnp.broadcast_to(mask[:, None], (hops, LANES))

        def fold(a):
            a = a.reshape(a.shape[:-1] + (q, LANES))
            if q8 > q:
                a = jnp.pad(a, [(0, 0)] * (a.ndim - 2) + [(0, q8 - q), (0, 0)])
            return a

        rates = fold(decay_rates)
        decay = jnp.exp(-rates)
        res = fold(residues)
        skip = fold(skip_gain)
        smem = pl.BlockSpec(memory_space=pltpu.SMEM)
        rows = pl.BlockSpec((chunk, channels), lambda i: (i, 0))
        whole = pl.BlockSpec((modes, q8, LANES), lambda i: (0, 0, 0))
        end = pl.pallas_call(
            functools.partial(end_state_kernel, modes, q, q8),
            grid=(length // chunk,),
            out_shape=jax.ShapeDtypeStruct((modes, q8, LANES), jnp.bfloat16),
            in_specs=[smem, rows, rows, whole],
            out_specs=whole,
            scratch_shapes=[
                pltpu.VMEM((chunk * q8, LANES), jnp.float32),
                pltpu.VMEM((modes, q8, LANES), jnp.float32),
            ],
            compiler_params=pltpu.CompilerParams(vmem_limit_bytes=16 << 20),
            name="end_state",
        )(last, gate_in, signal, decay)

        flat = (modes * q8, LANES)
        vmem = pl.BlockSpec(memory_space=pltpu.VMEM)
        carried = pl.pallas_call(
            functools.partial(exchange_kernel, n, length, plan),
            out_shape=jax.ShapeDtypeStruct(flat, jnp.float32),
            in_specs=[vmem] * 3,
            out_specs=vmem,
            scratch_shapes=[
                pltpu.VMEM((max(len(plan) - 1, 1),) + flat, jnp.bfloat16),
                pltpu.VMEM((hops,) + flat, jnp.bfloat16),
                pltpu.SemaphoreType.DMA((hops,)),
                pltpu.SemaphoreType.DMA((hops,)),
            ],
            compiler_params=pltpu.CompilerParams(
                collective_id=0, has_side_effects=True, vmem_limit_bytes=16 << 20
            ),
            name="state_exchange",
        )(end.reshape(flat), rates.reshape(flat), mask)

        hidden = pl.pallas_call(
            functools.partial(conv_kernel, modes, q, q8),
            grid=(length // chunk,),
            out_shape=jax.ShapeDtypeStruct((length, channels), jnp.bfloat16),
            in_specs=[smem, smem, rows, rows, rows, whole, whole,
                      pl.BlockSpec((q8, LANES), lambda i: (0, 0)), whole],
            out_specs=rows,
            scratch_shapes=[
                pltpu.VMEM((chunk * q8, LANES), jnp.float32),
                pltpu.VMEM((chunk * q8, LANES), jnp.float32),
                pltpu.VMEM((modes, q8, LANES), jnp.float32),
            ],
            compiler_params=pltpu.CompilerParams(vmem_limit_bytes=24 << 20),
            name="conv",
        )(keep, cut, gate_out, gate_in, signal, decay, res, skip,
          carried.reshape(modes, q8, LANES))

        def project(h):
            return jnp.dot(h, out_proj, preferred_element_type=jnp.float32).astype(jnp.bfloat16)

        if tp != 2:
            return lax.psum_scatter(project(hidden), "tp", scatter_dimension=0, tiled=True)
        half = length // 2
        core = lax.axis_index("tp")
        other = project(lax.dynamic_slice_in_dim(hidden, (1 - core) * half, half, 0))
        other = lax.ppermute(other, "tp", [(0, 1), (1, 0)])
        own = project(lax.dynamic_slice_in_dim(hidden, core * half, half, 0))
        return (own.astype(jnp.float32) + other.astype(jnp.float32)).astype(jnp.bfloat16)

    return per_device


def solution(mesh):
    return jax.shard_map(
        make(mesh.shape["ctx"], mesh.shape["tp"]),
        mesh=mesh,
        in_specs=(
            P("ctx", "tp"),
            P("ctx", "tp"),
            P("ctx", "tp"),
            P(None, "tp"),
            P(None, "tp"),
            P("tp"),
            P("tp", None),
            P(),
        ),
        out_specs=P(("ctx", "tp"), None),
        check_vma=False,
    )
```

```python
import functools

import jax
import jax.numpy as jnp
from jax import lax
from jax.experimental import pallas as pl
from jax.experimental.pallas import tpu as pltpu
from jax.sharding import PartitionSpec as P

LANES = 128
SUB = 8
STEP = 8
CHUNK = 64
TILE = 512
ROOM = 56 << 20


def fold(dst_ref, src_ref, q, q8, act):
    modes = src_ref.shape[0]
    if q8 > q:
        dst_ref[...] = jnp.zeros_like(dst_ref)
    for j in range(q):
        part = act(src_ref[:, pl.ds(j * LANES, LANES)])
        if modes == 1:
            dst_ref[pl.ds(j, 1), :] = part
        else:
            dst_ref[pl.ds(j, modes, stride=q8), :] = part


def mark(length, docs_ref, keep_ref, cut_ref, last_ref):
    begin = lax.axis_index("ctx") * length

    def clear(i, _):
        for k in range(STEP):
            keep_ref[i * STEP + k] = jnp.float32(1.0)
        cut_ref[i] = jnp.int32(0)
        return 0

    lax.fori_loop(0, length // STEP, clear, 0)
    last_ref[0] = jnp.int32(0)
    at = -begin
    for j in range(docs_ref.shape[0]):

        @pl.when((at >= 0) & (at < length))
        def _():
            keep_ref[at] = jnp.float32(0.0)
            cut_ref[lax.shift_right_logical(at, jnp.int32(STEP.bit_length() - 1))] = jnp.int32(1)
            last_ref[0] = at

        at = at + docs_ref[j]


def recur(modes, q8, h, rows, base, keep_ref, cut_ref, decay_ref, s_ref, x_ref, emit):
    d = [decay_ref[pl.ds(n * q8 + h, SUB), :] for n in range(modes)]

    def run(i, s, cut):
        s = list(s)
        for k in range(STEP):
            at = pl.multiple_of((i * STEP + k) * q8 + h, SUB)
            x = x_ref[pl.ds(at, SUB), :]
            if cut:
                keep = keep_ref[base + i * STEP + k]
                s = [keep * v for v in s]
            for n in range(modes):
                s[n] = d[n] * s[n] + x
            if emit is not None:
                emit(at, x, s)
        return tuple(s)

    def block(i, s):
        return lax.cond(
            cut_ref[base // STEP + i] > 0,
            lambda s: run(i, s, True),
            lambda s: run(i, s, False),
            s,
        )

    out = lax.fori_loop(
        0, rows // STEP, block, tuple(s_ref[pl.ds(n * q8 + h, SUB), :] for n in range(modes))
    )
    for n in range(modes):
        s_ref[pl.ds(n * q8 + h, SUB), :] = out[n]


def end_state_kernel(
    modes, q, q8, length, docs_ref, gate_ref, sig_ref, rates_ref, end_ref, x_ref,
    decay_ref, s_ref, keep_ref, cut_ref, last_ref,
):
    step = pl.program_id(0)
    rows = gate_ref.shape[0]

    @pl.when(step == 0)
    def _():
        s_ref[...] = jnp.zeros_like(s_ref)
        fold(decay_ref, rates_ref, q, q8, lambda a: jnp.exp(-a))
        mark(length, docs_ref, keep_ref, cut_ref, last_ref)

    def tile(i, _):
        t0 = pl.multiple_of(i * 16, 16)
        for j in range(q):
            cols = pl.ds(j * LANES, LANES)
            x = gate_ref[pl.ds(t0, 16), cols].astype(jnp.float32) * sig_ref[
                pl.ds(t0, 16), cols
            ].astype(jnp.float32)
            x_ref[pl.ds(t0 * q8 + j, 16, stride=q8), :] = x
        return 0

    lax.fori_loop(0, rows // 16, tile, 0)

    @pl.when((step + 1) * rows > last_ref[0])
    def _():
        for h in range(0, q8, SUB):
            recur(modes, q8, h, rows, step * rows, keep_ref, cut_ref, decay_ref, s_ref, x_ref, None)

    @pl.when(step == pl.num_programs(0) - 1)
    def _():
        end_ref[...] = s_ref[...].astype(end_ref.dtype)


def exchange_kernel(
    n, length, plan, q, q8, docs_ref, end_ref, rates_ref, out_ref, rate_ref, send_buf, slots,
    send_sem, recv_sem,
):
    me = lax.axis_index("ctx")
    offsets = sorted({off for stage in plan for off, _ in stage})
    barrier = pltpu.get_barrier_semaphore()
    for off in offsets:

        @pl.when(me >= off)
        def _():
            pl.semaphore_signal(
                barrier, inc=1, device_id={"ctx": me - off}, device_id_type=pl.DeviceIdType.MESH
            )

    peers = sum((me + off < n).astype(jnp.int32) for off in offsets)

    @pl.when(me + 1 < n)
    def _():
        pl.semaphore_wait(barrier, peers)

    def copy(k, stage, off):
        src = end_ref if stage == 0 else send_buf.at[stage - 1]
        return pltpu.make_async_remote_copy(
            src_ref=src,
            dst_ref=slots.at[k],
            send_sem=send_sem.at[k],
            recv_sem=recv_sem.at[k],
            device_id={"ctx": jnp.minimum(me + off, n - 1)},
            device_id_type=pl.DeviceIdType.MESH,
        )

    fold(rate_ref, rates_ref, q, q8, lambda a: a)
    start = head = jnp.int32(0)
    for j in range(docs_ref.shape[0]):
        head = jnp.where(start <= me * length, jnp.maximum(head, start), head)
        start = start + docs_ref[j]
    out_ref[...] = jnp.zeros_like(out_ref)
    k0 = 0
    for stage, hops in enumerate(plan):
        if stage:
            send_buf[stage - 1] = out_ref[...].astype(send_buf.dtype)
        for k, (off, gap) in enumerate(hops, k0):

            @pl.when(me + off < n)
            def _():
                copy(k, stage, off).start()

        for k, (off, gap) in enumerate(hops, k0):

            @pl.when(me >= off)
            def _():
                live = jnp.where(head < (me - gap) * length, 1.0, 0.0).astype(jnp.float32)
                weight = jnp.exp(rate_ref[...] * (-float(length * gap))) * live
                copy(k, stage, off).wait_recv()
                out_ref[...] += weight * slots[k].astype(jnp.float32)

        k0 += len(hops)
    k = 0
    for stage, hops in enumerate(plan):
        for off, gap in hops:

            @pl.when(me + off < n)
            def _():
                copy(k, stage, off).wait_send()

            k += 1


def conv_kernel(
    modes, q, q8, length, docs_ref, go_ref, x_ref, rates_ref, res_ref, gain_ref, carried_ref,
    hidden_ref, decay_ref, weight_ref, skip_ref, y_ref, s_ref, keep_ref, cut_ref, last_ref,
):
    step = pl.program_id(0)
    rows = go_ref.shape[0]

    @pl.when(step == 0)
    def _():
        s_ref[...] = carried_ref[...]
        fold(decay_ref, rates_ref, q, q8, lambda a: jnp.exp(-a))
        fold(weight_ref, res_ref, q, q8, lambda a: a)
        fold(skip_ref, gain_ref, q, q8, lambda a: a)
        mark(length, docs_ref, keep_ref, cut_ref, last_ref)

    for h in range(0, q8, SUB):
        r = [weight_ref[pl.ds(n * q8 + h, SUB), :] for n in range(modes)]
        skip = skip_ref[pl.ds(h, SUB), :]

        def emit(at, x, s):
            parts = [skip * x, None, None, None]
            for n in range(modes):
                term = r[n] * s[n]
                p = parts[n % 4]
                parts[n % 4] = term if p is None else p + term
            y_ref[pl.ds(at, SUB), :] = (parts[0] + parts[1]) + (parts[2] + parts[3])

        recur(modes, q8, h, rows, step * rows, keep_ref, cut_ref, decay_ref, s_ref, x_ref, emit)

    def tile(i, _):
        t0 = pl.multiple_of(i * 16, 16)
        for j in range(q):
            cols = pl.ds(j * LANES, LANES)
            y = y_ref[pl.ds(t0 * q8 + j, 16, stride=q8), :]
            g = go_ref[pl.ds(t0, 16), cols].astype(jnp.float32)
            hidden_ref[pl.ds(t0, 16), cols] = (g * y).astype(hidden_ref.dtype)
        return 0

    lax.fori_loop(0, rows // 16, tile, 0)


def project_kernel(hidden_ref, w_ref, out_ref, own_buf, send_buf, recv_buf, send_sem, recv_sem):
    j = pl.program_id(0)
    tiles = own_buf.shape[0]
    half = own_buf.shape[1]
    tile = own_buf.shape[2]
    core = lax.axis_index("tp")

    @pl.when(j == 0)
    def _():
        barrier = pltpu.get_barrier_semaphore()
        pl.semaphore_signal(
            barrier, inc=1, device_id={"tp": 1 - core}, device_id_type=pl.DeviceIdType.MESH
        )
        pl.semaphore_wait(barrier, 1)

    def copy(k):
        return pltpu.make_async_remote_copy(
            src_ref=send_buf.at[k],
            dst_ref=recv_buf.at[k],
            send_sem=send_sem.at[k],
            recv_sem=recv_sem.at[k],
            device_id={"tp": 1 - core},
            device_id_type=pl.DeviceIdType.MESH,
        )

    def product(side):
        rows = pl.ds(pl.multiple_of(side * half, half), half)
        return jnp.dot(
            hidden_ref[rows, :], w_ref[...], preferred_element_type=jnp.float32
        ).astype(jnp.bfloat16)

    def finish(k):
        copy(k).wait_recv()
        out_ref[:, pl.ds(pl.multiple_of(k * tile, tile), tile)] = (
            own_buf[k].astype(jnp.float32) + recv_buf[k].astype(jnp.float32)
        ).astype(out_ref.dtype)

    send_buf[j] = product(1 - core)
    copy(j).start()
    own_buf[j] = product(core)

    @pl.when(j > 0)
    def _():
        finish(j - 1)

    @pl.when(j == tiles - 1)
    def _():
        finish(j)

        def drain(k, _):
            copy(k).wait_send()
            return 0

        lax.fori_loop(0, tiles, drain, 0)


def scan_plan(n):
    plan = [[(off, off - 1) for off in range(1, min(4, n - 1) + 1)]]
    unit = 4
    while unit < n:
        plan.append([(off, off) for off in (unit, 2 * unit, 3 * unit) if off < n])
        unit *= 4
    return plan


def make(n, tp):
    plan = scan_plan(n)
    hops = sum(len(stage) for stage in plan)

    def per_device(gate_out, gate_in, signal, decay_rates, residues, skip_gain, out_proj, doc_lengths):
        length, channels = signal.shape
        modes = decay_rates.shape[0]
        width = out_proj.shape[1]
        q = channels // LANES
        q8 = -(-q // SUB) * SUB
        chunk = min(CHUNK, length)
        flat = (modes * q8, LANES)
        params = pltpu.CompilerParams(vmem_limit_bytes=ROOM)
        smem = pl.BlockSpec(memory_space=pltpu.SMEM)
        vmem = pl.BlockSpec(memory_space=pltpu.VMEM)
        rows = pl.BlockSpec((chunk, channels), lambda i: (i, 0))
        folded = pl.BlockSpec((chunk * q8, LANES), lambda i: (i, 0))
        table = pl.BlockSpec((modes, channels), lambda i: (0, 0))
        state = pl.BlockSpec(flat, lambda i: (0, 0))
        flags = [
            pltpu.SMEM((length,), jnp.float32),
            pltpu.SMEM((length // STEP,), jnp.int32),
            pltpu.SMEM((1,), jnp.int32),
        ]
        end, feed = pl.pallas_call(
            functools.partial(end_state_kernel, modes, q, q8, length),
            grid=(length // chunk,),
            out_shape=[
                jax.ShapeDtypeStruct(flat, jnp.bfloat16),
                jax.ShapeDtypeStruct((length * q8, LANES), jnp.float32),
            ],
            in_specs=[smem, rows, rows, table],
            out_specs=[state, folded],
            scratch_shapes=[pltpu.VMEM(flat, jnp.float32), pltpu.VMEM(flat, jnp.float32)] + flags,
            compiler_params=params,
            name="end_state",
        )(doc_lengths, gate_in, signal, decay_rates)

        carried = pl.pallas_call(
            functools.partial(exchange_kernel, n, length, plan, q, q8),
            out_shape=jax.ShapeDtypeStruct(flat, jnp.float32),
            in_specs=[smem, vmem, vmem],
            out_specs=vmem,
            scratch_shapes=[
                pltpu.VMEM(flat, jnp.float32),
                pltpu.VMEM((max(len(plan) - 1, 1),) + flat, jnp.bfloat16),
                pltpu.VMEM((hops,) + flat, jnp.bfloat16),
                pltpu.SemaphoreType.DMA((hops,)),
                pltpu.SemaphoreType.DMA((hops,)),
            ],
            compiler_params=pltpu.CompilerParams(
                collective_id=0, has_side_effects=True, vmem_limit_bytes=ROOM
            ),
            name="state_exchange",
        )(doc_lengths, end, decay_rates)

        hidden = pl.pallas_call(
            functools.partial(conv_kernel, modes, q, q8, length),
            grid=(length // chunk,),
            out_shape=jax.ShapeDtypeStruct((length, channels), jnp.bfloat16),
            in_specs=[smem, rows, folded, table, table,
                      pl.BlockSpec((1, channels), lambda i: (0, 0)), state],
            out_specs=rows,
            scratch_shapes=[
                pltpu.VMEM(flat, jnp.float32),
                pltpu.VMEM(flat, jnp.float32),
                pltpu.VMEM((q8, LANES), jnp.float32),
                pltpu.VMEM((chunk * q8, LANES), jnp.float32),
                pltpu.VMEM(flat, jnp.float32),
            ] + flags,
            compiler_params=params,
            name="conv",
        )(doc_lengths, gate_out, feed, decay_rates, residues, skip_gain.reshape(1, channels), carried)

        if tp != 2:
            part = jnp.dot(hidden, out_proj, preferred_element_type=jnp.float32)
            return lax.psum_scatter(
                part.astype(jnp.bfloat16), "tp", scatter_dimension=0, tiled=True
            )
        half = length // 2
        tile = min(TILE, width)
        tiles = width // tile
        return pl.pallas_call(
            project_kernel,
            grid=(tiles,),
            out_shape=jax.ShapeDtypeStruct((half, width), jnp.bfloat16),
            in_specs=[
                pl.BlockSpec((length, channels), lambda j: (0, 0)),
                pl.BlockSpec((channels, tile), lambda j: (0, j)),
            ],
            out_specs=pl.BlockSpec((half, width), lambda j: (0, 0)),
            scratch_shapes=[pltpu.VMEM((tiles, half, tile), jnp.bfloat16) for _ in range(3)]
            + [pltpu.SemaphoreType.DMA((tiles,)), pltpu.SemaphoreType.DMA((tiles,))],
            compiler_params=pltpu.CompilerParams(
                collective_id=1, has_side_effects=True, vmem_limit_bytes=ROOM
            ),
            name="project",
        )(hidden, out_proj)

    return per_device


def solution(mesh):
    return jax.shard_map(
        make(mesh.shape["ctx"], mesh.shape["tp"]),
        mesh=mesh,
        in_specs=(
            P("ctx", "tp"),
            P("ctx", "tp"),
            P("ctx", "tp"),
            P(None, "tp"),
            P(None, "tp"),
            P("tp"),
            P("tp", None),
            P(),
        ),
        out_specs=P(("ctx", "tp"), None),
        check_vma=False,
    )
```

```python
import functools

import jax
import jax.numpy as jnp
from jax import lax
from jax.experimental import pallas as pl
from jax.experimental.pallas import tpu as pltpu
from jax.sharding import PartitionSpec as P

LANES = 128
SUB = 8
STEP = 8
CHUNK = 128
SPAN = 64
TILE = 512
ROOM = 56 << 20


def fold(dst_ref, src_ref, q, q8, act):
    modes = src_ref.shape[0]
    if q8 > q:
        dst_ref[...] = jnp.zeros_like(dst_ref)
    for j in range(q):
        part = act(src_ref[:, pl.ds(j * LANES, LANES)])
        if modes == 1:
            dst_ref[pl.ds(j, 1), :] = part
        else:
            dst_ref[pl.ds(j, modes, stride=q8), :] = part


def opens(docs_ref, begin, rows):
    hit = jnp.int32(0)
    at = -begin
    for j in range(docs_ref.shape[0]):
        hit = jnp.where((at >= 0) & (at < rows), jnp.int32(1), hit)
        at = at + docs_ref[j]
    return hit > 0


def mark(docs_ref, begin, rows, keep_ref):
    def clear(i, _):
        for k in range(STEP):
            keep_ref[i * STEP + k] = jnp.float32(1.0)
        return 0

    lax.fori_loop(0, rows // STEP, clear, 0)
    at = -begin
    for j in range(docs_ref.shape[0]):

        @pl.when((at >= 0) & (at < rows))
        def _():
            keep_ref[at] = jnp.float32(0.0)

        at = at + docs_ref[j]


def recur(modes, q8, span, row0, begin, docs_ref, keep_ref, decay_ref, s_ref, x_ref, emitter):
    def sweep(cut):
        for h in range(0, q8, SUB):
            d = [decay_ref[pl.ds(n * q8 + h, SUB), :] for n in range(modes)]
            emit = emitter(h)

            def run(i, s):
                s = list(s)
                for k in range(STEP):
                    at = pl.multiple_of((row0 + i * STEP + k) * q8 + h, SUB)
                    x = x_ref[pl.ds(at, SUB), :]
                    if cut:
                        keep = keep_ref[i * STEP + k]
                        s = [keep * v for v in s]
                    for n in range(modes):
                        s[n] = d[n] * s[n] + x
                    if emit is not None:
                        emit(at, x, s)
                return tuple(s)

            out = lax.fori_loop(
                0,
                span // STEP,
                run,
                tuple(s_ref[pl.ds(n * q8 + h, SUB), :] for n in range(modes)),
            )
            for n in range(modes):
                s_ref[pl.ds(n * q8 + h, SUB), :] = out[n]

    hit = opens(docs_ref, begin, span)

    @pl.when(hit)
    def _():
        mark(docs_ref, begin, span, keep_ref)
        sweep(True)

    @pl.when(jnp.logical_not(hit))
    def _():
        sweep(False)


def end_state_kernel(
    modes, q, q8, length, docs_ref, gate_ref, sig_ref, rates_ref, end_ref, x_ref, decay_ref,
    s_ref, keep_ref,
):
    step = pl.program_id(0)
    rows = gate_ref.shape[0]

    @pl.when(step == 0)
    def _():
        s_ref[...] = jnp.zeros_like(s_ref)
        fold(decay_ref, rates_ref, q, q8, lambda a: jnp.exp(-a))

    def tile(i, _):
        t0 = pl.multiple_of(i * 16, 16)
        for j in range(q):
            cols = pl.ds(j * LANES, LANES)
            x = gate_ref[pl.ds(t0, 16), cols].astype(jnp.float32) * sig_ref[
                pl.ds(t0, 16), cols
            ].astype(jnp.float32)
            x_ref[pl.ds(t0 * q8 + j, 16, stride=q8), :] = x
        return 0

    lax.fori_loop(0, rows // 16, tile, 0)

    begin = lax.axis_index("ctx") * length
    span = min(SPAN, rows)
    last = at = -begin
    for j in range(docs_ref.shape[0]):
        last = jnp.where(at < length, at, last)
        at = at + docs_ref[j]

    def piece(p, _):
        first = step * rows + p * span

        @pl.when(first + span > last)
        def _():
            recur(
                modes, q8, span, p * span, begin + first, docs_ref, keep_ref, decay_ref, s_ref,
                x_ref, lambda h: None,
            )

        return 0

    lax.fori_loop(0, rows // span, piece, 0)

    @pl.when(step == pl.num_programs(0) - 1)
    def _():
        end_ref[...] = s_ref[...].astype(end_ref.dtype)


def exchange_kernel(
    n, length, plan, q, q8, docs_ref, end_ref, rates_ref, out_ref, rate_ref, send_buf, slots,
    send_sem, recv_sem,
):
    me = lax.axis_index("ctx")
    offsets = sorted({off for stage in plan for off, _ in stage})
    barrier = pltpu.get_barrier_semaphore()
    for off in offsets:

        @pl.when(me >= off)
        def _():
            pl.semaphore_signal(
                barrier, inc=1, device_id={"ctx": me - off}, device_id_type=pl.DeviceIdType.MESH
            )

    peers = sum((me + off < n).astype(jnp.int32) for off in offsets)

    @pl.when(me + 1 < n)
    def _():
        pl.semaphore_wait(barrier, peers)

    def copy(k, stage, off):
        src = end_ref if stage == 0 else send_buf.at[stage - 1]
        return pltpu.make_async_remote_copy(
            src_ref=src,
            dst_ref=slots.at[k],
            send_sem=send_sem.at[k],
            recv_sem=recv_sem.at[k],
            device_id={"ctx": jnp.minimum(me + off, n - 1)},
            device_id_type=pl.DeviceIdType.MESH,
        )

    fold(rate_ref, rates_ref, q, q8, lambda a: a)
    start = head = jnp.int32(0)
    for j in range(docs_ref.shape[0]):
        head = jnp.where(start <= me * length, jnp.maximum(head, start), head)
        start = start + docs_ref[j]
    out_ref[...] = jnp.zeros_like(out_ref)
    k0 = 0
    for stage, hops in enumerate(plan):
        if stage:
            send_buf[stage - 1] = out_ref[...].astype(send_buf.dtype)
        for k, (off, gap) in enumerate(hops, k0):

            @pl.when(me + off < n)
            def _():
                copy(k, stage, off).start()

        for k, (off, gap) in enumerate(hops, k0):

            @pl.when(me >= off)
            def _():
                live = jnp.where(head < (me - gap) * length, 1.0, 0.0).astype(jnp.float32)
                weight = jnp.exp(rate_ref[...] * (-float(length * gap))) * live
                copy(k, stage, off).wait_recv()
                out_ref[...] += weight * slots[k].astype(jnp.float32)

        k0 += len(hops)
    k = 0
    for stage, hops in enumerate(plan):
        for off, gap in hops:

            @pl.when(me + off < n)
            def _():
                copy(k, stage, off).wait_send()

            k += 1


def conv_kernel(
    modes, q, q8, length, docs_ref, go_ref, x_ref, decay_ref, res_ref, gain_ref, carried_ref,
    hidden_ref, weight_ref, skip_ref, y_ref, s_ref, keep_ref,
):
    step = pl.program_id(0)
    rows = go_ref.shape[0]

    @pl.when(step == 0)
    def _():
        s_ref[...] = carried_ref[...]
        fold(weight_ref, res_ref, q, q8, lambda a: a)
        fold(skip_ref, gain_ref, q, q8, lambda a: a)

    def emitter(h):
        r = [weight_ref[pl.ds(n * q8 + h, SUB), :] for n in range(modes)]
        skip = skip_ref[pl.ds(h, SUB), :]

        def emit(at, x, s):
            parts = [skip * x, None, None, None]
            for n in range(modes):
                term = r[n] * s[n]
                p = parts[n % 4]
                parts[n % 4] = term if p is None else p + term
            y_ref[pl.ds(at, SUB), :] = (parts[0] + parts[1]) + (parts[2] + parts[3])

        return emit

    span = min(SPAN, rows)
    begin = lax.axis_index("ctx") * length + step * rows

    def piece(p, _):
        recur(
            modes, q8, span, p * span, begin + p * span, docs_ref, keep_ref, decay_ref, s_ref,
            x_ref, emitter,
        )
        return 0

    lax.fori_loop(0, rows // span, piece, 0)

    def tile(i, _):
        t0 = pl.multiple_of(i * 16, 16)
        for j in range(q):
            cols = pl.ds(j * LANES, LANES)
            y = y_ref[pl.ds(t0 * q8 + j, 16, stride=q8), :]
            g = go_ref[pl.ds(t0, 16), cols].astype(jnp.float32)
            hidden_ref[pl.ds(t0, 16), cols] = (g * y).astype(hidden_ref.dtype)
        return 0

    lax.fori_loop(0, rows // 16, tile, 0)


def project_kernel(
    hidden_ref, w_ref, out_ref, part_ref, own_buf, send_buf, recv_buf, send_sem, recv_sem
):
    j = pl.program_id(0)
    tiles = own_buf.shape[0]
    half = own_buf.shape[1]
    tile = own_buf.shape[2]
    core = lax.axis_index("tp")

    @pl.when(j == 0)
    def _():
        barrier = pltpu.get_barrier_semaphore()
        pl.semaphore_signal(
            barrier, inc=1, device_id={"tp": 1 - core}, device_id_type=pl.DeviceIdType.MESH
        )
        pl.semaphore_wait(barrier, 1)

    def copy(k):
        return pltpu.make_async_remote_copy(
            src_ref=send_buf.at[k],
            dst_ref=recv_buf.at[k],
            send_sem=send_sem.at[k],
            recv_sem=recv_sem.at[k],
            device_id={"tp": 1 - core},
            device_id_type=pl.DeviceIdType.MESH,
        )

    def finish(k):
        copy(k).wait_recv()
        out_ref[:, pl.ds(pl.multiple_of(k * tile, tile), tile)] = (
            own_buf[k].astype(jnp.float32) + recv_buf[k].astype(jnp.float32)
        ).astype(out_ref.dtype)

    part_ref[...] = jnp.dot(
        hidden_ref[...], w_ref[...], preferred_element_type=jnp.float32
    ).astype(part_ref.dtype)
    send_buf[j] = part_ref[pl.ds(pl.multiple_of((1 - core) * half, half), half), :]
    copy(j).start()
    own_buf[j] = part_ref[pl.ds(pl.multiple_of(core * half, half), half), :]

    @pl.when(j > 0)
    def _():
        finish(j - 1)

    @pl.when(j == tiles - 1)
    def _():
        finish(j)

        def drain(k, _):
            copy(k).wait_send()
            return 0

        lax.fori_loop(0, tiles, drain, 0)


def scan_plan(n, reach):
    plan = [[(off, off - 1) for off in range(1, min(4, n - 1) + 1)]]
    unit = 4
    while unit < n:
        plan.append([(off, off) for off in (unit, 2 * unit, 3 * unit) if off < min(n, reach)])
        unit *= 4
    return plan


def make(n, tp):
    def per_device(gate_out, gate_in, signal, decay_rates, residues, skip_gain, out_proj, doc_lengths):
        length, channels = signal.shape
        modes = decay_rates.shape[0]
        width = out_proj.shape[1]
        q = channels // LANES
        q8 = -(-q // SUB) * SUB
        chunk = min(CHUNK, length)
        flat = (modes * q8, LANES)
        params = pltpu.CompilerParams(vmem_limit_bytes=ROOM)
        smem = pl.BlockSpec(memory_space=pltpu.SMEM)
        vmem = pl.BlockSpec(memory_space=pltpu.VMEM)
        rows = pl.BlockSpec((chunk, channels), lambda i: (i, 0))
        folded = pl.BlockSpec((chunk * q8, LANES), lambda i: (i, 0))
        table = pl.BlockSpec((modes, channels), lambda i: (0, 0))
        state = pl.BlockSpec(flat, lambda i: (0, 0))
        plan = scan_plan(n, -(-(5 * n * length // 8) // length))
        hops = sum(len(stage) for stage in plan)
        flags = [pltpu.SMEM((SPAN,), jnp.float32)]
        end, feed, decay = pl.pallas_call(
            functools.partial(end_state_kernel, modes, q, q8, length),
            grid=(length // chunk,),
            out_shape=[
                jax.ShapeDtypeStruct(flat, jnp.bfloat16),
                jax.ShapeDtypeStruct((length * q8, LANES), jnp.float32),
                jax.ShapeDtypeStruct(flat, jnp.float32),
            ],
            in_specs=[smem, rows, rows, table],
            out_specs=[state, folded, state],
            scratch_shapes=[pltpu.VMEM(flat, jnp.float32)] + flags,
            compiler_params=params,
            name="end_state",
        )(doc_lengths, gate_in, signal, decay_rates)

        carried = pl.pallas_call(
            functools.partial(exchange_kernel, n, length, plan, q, q8),
            out_shape=jax.ShapeDtypeStruct(flat, jnp.float32),
            in_specs=[smem, vmem, vmem],
            out_specs=vmem,
            scratch_shapes=[
                pltpu.VMEM(flat, jnp.float32),
                pltpu.VMEM((max(len(plan) - 1, 1),) + flat, jnp.bfloat16),
                pltpu.VMEM((hops,) + flat, jnp.bfloat16),
                pltpu.SemaphoreType.DMA((hops,)),
                pltpu.SemaphoreType.DMA((hops,)),
            ],
            compiler_params=pltpu.CompilerParams(
                collective_id=0, has_side_effects=True, vmem_limit_bytes=ROOM
            ),
            name="state_exchange",
        )(doc_lengths, end, decay_rates)

        hidden = pl.pallas_call(
            functools.partial(conv_kernel, modes, q, q8, length),
            grid=(length // chunk,),
            out_shape=jax.ShapeDtypeStruct((length, channels), jnp.bfloat16),
            in_specs=[smem, rows, folded, state, table,
                      pl.BlockSpec((1, channels), lambda i: (0, 0)), state],
            out_specs=rows,
            scratch_shapes=[
                pltpu.VMEM(flat, jnp.float32),
                pltpu.VMEM((q8, LANES), jnp.float32),
                pltpu.VMEM((chunk * q8, LANES), jnp.float32),
                pltpu.VMEM(flat, jnp.float32),
            ] + flags,
            compiler_params=params,
            name="conv",
        )(doc_lengths, gate_out, feed, decay, residues, skip_gain.reshape(1, channels), carried)

        if tp != 2:
            part = jnp.dot(hidden, out_proj, preferred_element_type=jnp.float32)
            return lax.psum_scatter(
                part.astype(jnp.bfloat16), "tp", scatter_dimension=0, tiled=True
            )
        half = length // 2
        tile = min(TILE, width)
        tiles = width // tile
        return pl.pallas_call(
            project_kernel,
            grid=(tiles,),
            out_shape=jax.ShapeDtypeStruct((half, width), jnp.bfloat16),
            in_specs=[
                pl.BlockSpec((length, channels), lambda j: (0, 0)),
                pl.BlockSpec((channels, tile), lambda j: (0, j)),
            ],
            out_specs=pl.BlockSpec((half, width), lambda j: (0, 0)),
            scratch_shapes=[pltpu.VMEM((length, tile), jnp.bfloat16)]
            + [pltpu.VMEM((tiles, half, tile), jnp.bfloat16) for _ in range(3)]
            + [pltpu.SemaphoreType.DMA((tiles,)), pltpu.SemaphoreType.DMA((tiles,))],
            compiler_params=pltpu.CompilerParams(
                collective_id=1, has_side_effects=True, vmem_limit_bytes=ROOM
            ),
            name="project",
        )(hidden, out_proj)

    return per_device


def solution(mesh):
    return jax.shard_map(
        make(mesh.shape["ctx"], mesh.shape["tp"]),
        mesh=mesh,
        in_specs=(
            P("ctx", "tp"),
            P("ctx", "tp"),
            P("ctx", "tp"),
            P(None, "tp"),
            P(None, "tp"),
            P("tp"),
            P("tp", None),
            P(),
        ),
        out_specs=P(("ctx", "tp"), None),
        check_vma=False,
    )
```

```python
import functools

import jax
import jax.numpy as jnp
from jax import lax
from jax.experimental import pallas as pl
from jax.experimental.pallas import tpu as pltpu
from jax.sharding import PartitionSpec as P

LANES = 128
SUB = 8
STEP = 8
CHUNK = 128
SPAN = 64
TILE = 512
ROOM = 56 << 20
ROOM_CONV = 40 << 20
ROOM_OUT = 16 << 20


def fold(dst_ref, src_ref, q, q8, act):
    modes = src_ref.shape[0]
    if q8 > q:
        dst_ref[...] = jnp.zeros_like(dst_ref)
    for j in range(q):
        part = act(src_ref[:, pl.ds(j * LANES, LANES)])
        if modes == 1:
            dst_ref[pl.ds(j, 1), :] = part
        else:
            dst_ref[pl.ds(j, modes, stride=q8), :] = part


def opens(docs_ref, begin, rows):
    hit = jnp.int32(0)
    at = -begin
    for j in range(docs_ref.shape[0]):
        hit = jnp.where((at >= 0) & (at < rows), jnp.int32(1), hit)
        at = at + docs_ref[j]
    return hit > 0


def mark(docs_ref, begin, rows, keep_ref):
    def clear(i, _):
        for k in range(STEP):
            keep_ref[i * STEP + k] = jnp.float32(1.0)
        return 0

    lax.fori_loop(0, rows // STEP, clear, 0)
    at = -begin
    for j in range(docs_ref.shape[0]):

        @pl.when((at >= 0) & (at < rows))
        def _():
            keep_ref[at] = jnp.float32(0.0)

        at = at + docs_ref[j]


def recur(modes, q8, span, row0, begin, docs_ref, keep_ref, decay_ref, s_ref, x_ref, emitter):
    def sweep(cut):
        for h in range(0, q8, SUB):
            d = [decay_ref[pl.ds(n * q8 + h, SUB), :] for n in range(modes)]
            emit = emitter(h)

            def run(i, s):
                s = list(s)
                for k in range(STEP):
                    at = pl.multiple_of((row0 + i * STEP + k) * q8 + h, SUB)
                    x = x_ref[pl.ds(at, SUB), :]
                    if cut:
                        keep = keep_ref[i * STEP + k]
                        s = [keep * v for v in s]
                    for n in range(modes):
                        s[n] = d[n] * s[n] + x
                    if emit is not None:
                        emit(at, x, s)
                return tuple(s)

            out = lax.fori_loop(
                0,
                span // STEP,
                run,
                tuple(s_ref[pl.ds(n * q8 + h, SUB), :] for n in range(modes)),
            )
            for n in range(modes):
                s_ref[pl.ds(n * q8 + h, SUB), :] = out[n]

    hit = opens(docs_ref, begin, span)

    @pl.when(hit)
    def _():
        mark(docs_ref, begin, span, keep_ref)
        sweep(True)

    @pl.when(jnp.logical_not(hit))
    def _():
        sweep(False)


def end_state_kernel(
    modes, q, q8, length, docs_ref, gate_ref, sig_ref, rates_ref, end_ref, x_ref, decay_ref,
    s_ref, keep_ref,
):
    step = pl.program_id(0)
    rows = gate_ref.shape[0]

    @pl.when(step == 0)
    def _():
        s_ref[...] = jnp.zeros_like(s_ref)
        fold(decay_ref, rates_ref, q, q8, lambda a: jnp.exp(-a))

    def tile(i, _):
        t0 = pl.multiple_of(i * 16, 16)
        for j in range(q):
            cols = pl.ds(j * LANES, LANES)
            x = gate_ref[pl.ds(t0, 16), cols].astype(jnp.float32) * sig_ref[
                pl.ds(t0, 16), cols
            ].astype(jnp.float32)
            x_ref[pl.ds(t0 * q8 + j, 16, stride=q8), :] = x
        return 0

    lax.fori_loop(0, rows // 16, tile, 0)

    begin = lax.axis_index("ctx") * length
    span = min(SPAN, rows)
    last = at = -begin
    for j in range(docs_ref.shape[0]):
        last = jnp.where(at < length, at, last)
        at = at + docs_ref[j]

    def piece(p, _):
        first = step * rows + p * span

        @pl.when(first + span > last)
        def _():
            recur(
                modes, q8, span, p * span, begin + first, docs_ref, keep_ref, decay_ref, s_ref,
                x_ref, lambda h: None,
            )

        return 0

    lax.fori_loop(0, rows // span, piece, 0)

    @pl.when(step == pl.num_programs(0) - 1)
    def _():
        end_ref[...] = s_ref[...].astype(end_ref.dtype)


def exchange_kernel(
    n, length, plan, q, q8, docs_ref, end_ref, rates_ref, out_ref, rate_ref, send_buf, slots,
    send_sem, recv_sem,
):
    me = lax.axis_index("ctx")
    offsets = sorted({off for stage in plan for off, _ in stage})
    barrier = pltpu.get_barrier_semaphore()
    for off in offsets:

        @pl.when(me >= off)
        def _():
            pl.semaphore_signal(
                barrier, inc=1, device_id={"ctx": me - off}, device_id_type=pl.DeviceIdType.MESH
            )

    peers = sum((me + off < n).astype(jnp.int32) for off in offsets)

    @pl.when(me + 1 < n)
    def _():
        pl.semaphore_wait(barrier, peers)

    def copy(k, stage, off):
        src = end_ref if stage == 0 else send_buf.at[stage - 1]
        return pltpu.make_async_remote_copy(
            src_ref=src,
            dst_ref=slots.at[k],
            send_sem=send_sem.at[k],
            recv_sem=recv_sem.at[k],
            device_id={"ctx": jnp.minimum(me + off, n - 1)},
            device_id_type=pl.DeviceIdType.MESH,
        )

    fold(rate_ref, rates_ref, q, q8, lambda a: a)
    start = head = jnp.int32(0)
    for j in range(docs_ref.shape[0]):
        head = jnp.where(start <= me * length, jnp.maximum(head, start), head)
        start = start + docs_ref[j]
    out_ref[...] = jnp.zeros_like(out_ref)
    k0 = 0
    for stage, hops in enumerate(plan):
        if stage:
            send_buf[stage - 1] = out_ref[...].astype(send_buf.dtype)
        for k, (off, gap) in enumerate(hops, k0):

            @pl.when(me + off < n)
            def _():
                copy(k, stage, off).start()

        for k, (off, gap) in enumerate(hops, k0):

            @pl.when(me >= off)
            def _():
                live = jnp.where(head < (me - gap) * length, 1.0, 0.0).astype(jnp.float32)
                weight = jnp.exp(rate_ref[...] * (-float(length * gap))) * live
                copy(k, stage, off).wait_recv()
                out_ref[...] += weight * slots[k].astype(jnp.float32)

        k0 += len(hops)
    k = 0
    for stage, hops in enumerate(plan):
        for off, gap in hops:

            @pl.when(me + off < n)
            def _():
                copy(k, stage, off).wait_send()

            k += 1


def conv_kernel(
    modes, q, q8, length, docs_ref, go_ref, x_ref, decay_ref, res_ref, gain_ref, carried_ref,
    w_ref, hidden_ref, near_ref, weight_ref, skip_ref, y_ref, s_ref, keep_ref, w_sem,
):
    step = pl.program_id(0)
    rows = go_ref.shape[0]
    fetch = pltpu.make_async_copy(w_ref, near_ref, w_sem)
    pl.when(step == 0)(fetch.start)

    @pl.when(step == 0)
    def _():
        s_ref[...] = carried_ref[...]
        fold(weight_ref, res_ref, q, q8, lambda a: a)
        fold(skip_ref, gain_ref, q, q8, lambda a: a)

    def emitter(h):
        r = [weight_ref[pl.ds(n * q8 + h, SUB), :] for n in range(modes)]
        skip = skip_ref[pl.ds(h, SUB), :]

        def emit(at, x, s):
            parts = [skip * x, None, None, None]
            for n in range(modes):
                term = r[n] * s[n]
                p = parts[n % 4]
                parts[n % 4] = term if p is None else p + term
            y_ref[pl.ds(at, SUB), :] = (parts[0] + parts[1]) + (parts[2] + parts[3])

        return emit

    span = min(SPAN, rows)
    begin = lax.axis_index("ctx") * length + step * rows

    def piece(p, _):
        recur(
            modes, q8, span, p * span, begin + p * span, docs_ref, keep_ref, decay_ref, s_ref,
            x_ref, emitter,
        )
        return 0

    lax.fori_loop(0, rows // span, piece, 0)

    def tile(i, _):
        t0 = pl.multiple_of(i * 16, 16)
        for j in range(q):
            cols = pl.ds(j * LANES, LANES)
            y = y_ref[pl.ds(t0 * q8 + j, 16, stride=q8), :]
            g = go_ref[pl.ds(t0, 16), cols].astype(jnp.float32)
            hidden_ref[pl.ds(t0, 16), cols] = (g * y).astype(hidden_ref.dtype)
        return 0

    lax.fori_loop(0, rows // 16, tile, 0)
    pl.when(step == pl.num_programs(0) - 1)(fetch.wait)


def project_kernel(
    hidden_ref, w_ref, out_ref, part_ref, own_buf, send_buf, recv_buf, send_sem, recv_sem
):
    tiles = own_buf.shape[0]
    half = own_buf.shape[1]
    tile = own_buf.shape[2]
    core = lax.axis_index("tp")
    barrier = pltpu.get_barrier_semaphore()
    pl.semaphore_signal(
        barrier, inc=1, device_id={"tp": 1 - core}, device_id_type=pl.DeviceIdType.MESH
    )
    pl.semaphore_wait(barrier, 1)

    def copy(k):
        return pltpu.make_async_remote_copy(
            src_ref=send_buf.at[k],
            dst_ref=recv_buf.at[k],
            send_sem=send_sem.at[k],
            recv_sem=recv_sem.at[k],
            device_id={"tp": 1 - core},
            device_id_type=pl.DeviceIdType.MESH,
        )

    def finish(k):
        copy(k).wait_recv()
        out_ref[:, pl.ds(pl.multiple_of(k * tile, tile), tile)] = (
            own_buf[k].astype(jnp.float32) + recv_buf[k].astype(jnp.float32)
        ).astype(out_ref.dtype)

    def step(j, _):
        cols = pl.ds(pl.multiple_of(j * tile, tile), tile)
        part_ref[...] = jnp.dot(
            hidden_ref[...], w_ref[:, cols], preferred_element_type=jnp.float32
        ).astype(part_ref.dtype)
        send_buf[j] = part_ref[pl.ds(pl.multiple_of((1 - core) * half, half), half), :]
        copy(j).start()
        own_buf[j] = part_ref[pl.ds(pl.multiple_of(core * half, half), half), :]

        @pl.when(j > 0)
        def _():
            finish(j - 1)

        return 0

    lax.fori_loop(0, tiles, step, 0)
    finish(tiles - 1)

    def drain(k, _):
        copy(k).wait_send()
        return 0

    lax.fori_loop(0, tiles, drain, 0)


def scan_plan(n, reach):
    plan = [[(off, off - 1) for off in range(1, min(4, n - 1) + 1)]]
    unit = 4
    while unit < n:
        plan.append([(off, off) for off in (unit, 2 * unit, 3 * unit) if off < min(n, reach)])
        unit *= 4
    return plan


def make(n, tp):
    def per_device(gate_out, gate_in, signal, decay_rates, residues, skip_gain, out_proj, doc_lengths):
        length, channels = signal.shape
        modes = decay_rates.shape[0]
        width = out_proj.shape[1]
        q = channels // LANES
        q8 = -(-q // SUB) * SUB
        chunk = min(CHUNK, length)
        flat = (modes * q8, LANES)
        params = pltpu.CompilerParams(vmem_limit_bytes=ROOM)
        smem = pl.BlockSpec(memory_space=pltpu.SMEM)
        vmem = pl.BlockSpec(memory_space=pltpu.VMEM)
        rows = pl.BlockSpec((chunk, channels), lambda i: (i, 0))
        folded = pl.BlockSpec((chunk * q8, LANES), lambda i: (i, 0))
        table = pl.BlockSpec((modes, channels), lambda i: (0, 0))
        state = pl.BlockSpec(flat, lambda i: (0, 0))
        plan = scan_plan(n, -(-(5 * n * length // 8) // length))
        hops = sum(len(stage) for stage in plan)
        flags = [pltpu.SMEM((SPAN,), jnp.float32)]
        end, feed, decay = pl.pallas_call(
            functools.partial(end_state_kernel, modes, q, q8, length),
            grid=(length // chunk,),
            out_shape=[
                jax.ShapeDtypeStruct(flat, jnp.bfloat16),
                jax.ShapeDtypeStruct((length * q8, LANES), jnp.float32),
                jax.ShapeDtypeStruct(flat, jnp.float32),
            ],
            in_specs=[smem, rows, rows, table],
            out_specs=[state, folded, state],
            scratch_shapes=[pltpu.VMEM(flat, jnp.float32)] + flags,
            compiler_params=params,
            name="end_state",
        )(doc_lengths, gate_in, signal, decay_rates)

        carried = pl.pallas_call(
            functools.partial(exchange_kernel, n, length, plan, q, q8),
            out_shape=jax.ShapeDtypeStruct(flat, jnp.float32),
            in_specs=[smem, vmem, vmem],
            out_specs=vmem,
            scratch_shapes=[
                pltpu.VMEM(flat, jnp.float32),
                pltpu.VMEM((max(len(plan) - 1, 1),) + flat, jnp.bfloat16),
                pltpu.VMEM((hops,) + flat, jnp.bfloat16),
                pltpu.SemaphoreType.DMA((hops,)),
                pltpu.SemaphoreType.DMA((hops,)),
            ],
            compiler_params=pltpu.CompilerParams(
                collective_id=0, has_side_effects=True, vmem_limit_bytes=ROOM
            ),
            name="state_exchange",
        )(doc_lengths, end, decay_rates)

        hidden, near = pl.pallas_call(
            functools.partial(conv_kernel, modes, q, q8, length),
            grid=(length // chunk,),
            out_shape=[
                pltpu.VMEM((length, channels), jnp.bfloat16),
                pltpu.VMEM(out_proj.shape, out_proj.dtype),
            ],
            in_specs=[smem, rows, folded, state, table,
                      pl.BlockSpec((1, channels), lambda i: (0, 0)), state,
                      pl.BlockSpec(memory_space=pltpu.HBM)],
            out_specs=[rows, pl.BlockSpec(memory_space=pl.ANY)],
            scratch_shapes=[
                pltpu.VMEM(flat, jnp.float32),
                pltpu.VMEM((q8, LANES), jnp.float32),
                pltpu.VMEM((chunk * q8, LANES), jnp.float32),
                pltpu.VMEM(flat, jnp.float32),
            ] + flags + [pltpu.SemaphoreType.DMA],
            compiler_params=pltpu.CompilerParams(vmem_limit_bytes=ROOM_CONV),
            name="conv",
        )(doc_lengths, gate_out, feed, decay, residues, skip_gain.reshape(1, channels), carried,
          out_proj)

        if tp != 2:
            part = jnp.dot(hidden, near, preferred_element_type=jnp.float32)
            return lax.psum_scatter(
                part.astype(jnp.bfloat16), "tp", scatter_dimension=0, tiled=True
            )
        half = length // 2
        tile = min(TILE, width)
        tiles = width // tile
        return pl.pallas_call(
            project_kernel,
            out_shape=jax.ShapeDtypeStruct((half, width), jnp.bfloat16),
            in_specs=[vmem, vmem],
            out_specs=vmem,
            scratch_shapes=[pltpu.VMEM((length, tile), jnp.bfloat16)]
            + [pltpu.VMEM((tiles, half, tile), jnp.bfloat16) for _ in range(3)]
            + [pltpu.SemaphoreType.DMA((tiles,)), pltpu.SemaphoreType.DMA((tiles,))],
            compiler_params=pltpu.CompilerParams(
                collective_id=1, has_side_effects=True, vmem_limit_bytes=ROOM_OUT
            ),
            name="project",
        )(hidden, near)

    return per_device


def solution(mesh):
    return jax.shard_map(
        make(mesh.shape["ctx"], mesh.shape["tp"]),
        mesh=mesh,
        in_specs=(
            P("ctx", "tp"),
            P("ctx", "tp"),
            P("ctx", "tp"),
            P(None, "tp"),
            P(None, "tp"),
            P("tp"),
            P("tp", None),
            P(),
        ),
        out_specs=P(("ctx", "tp"), None),
        check_vma=False,
    )
```

```python
import functools

import jax
import jax.numpy as jnp
from jax import lax
from jax.experimental import pallas as pl
from jax.experimental.pallas import tpu as pltpu
from jax.sharding import PartitionSpec as P

LANES = 128
SUB = 8
STEP = 16
CHUNK = 128
SPAN = 64
TILE = 512
ROOM = 56 << 20
ROOM_CONV = 40 << 20
ROOM_OUT = 16 << 20


def fold(dst_ref, src_ref, q, q8, act):
    modes = src_ref.shape[0]
    if q8 > q:
        dst_ref[...] = jnp.zeros_like(dst_ref)
    for j in range(q):
        part = act(src_ref[:, pl.ds(j * LANES, LANES)])
        if modes == 1:
            dst_ref[pl.ds(j, 1), :] = part
        else:
            dst_ref[pl.ds(j, modes, stride=q8), :] = part


def opens(docs_ref, begin, rows):
    hit = jnp.int32(0)
    at = -begin
    for j in range(docs_ref.shape[0]):
        hit = jnp.where((at >= 0) & (at < rows), jnp.int32(1), hit)
        at = at + docs_ref[j]
    return hit > 0


def mark(docs_ref, begin, rows, keep_ref):
    def clear(i, _):
        for k in range(STEP):
            keep_ref[i * STEP + k] = jnp.float32(1.0)
        return 0

    lax.fori_loop(0, rows // STEP, clear, 0)
    at = -begin
    for j in range(docs_ref.shape[0]):

        @pl.when((at >= 0) & (at < rows))
        def _():
            keep_ref[at] = jnp.float32(0.0)

        at = at + docs_ref[j]


def recur(modes, q8, span, row0, begin, docs_ref, keep_ref, decay_ref, s_ref, x_ref, emitter):
    def sweep(cut):
        for h in range(0, q8, SUB):
            d = [decay_ref[pl.ds(n * q8 + h, SUB), :] for n in range(modes)]
            emit = emitter(h)

            def run(i, s):
                s = list(s)
                for k in range(STEP):
                    at = pl.multiple_of((row0 + i * STEP + k) * q8 + h, SUB)
                    x = x_ref[pl.ds(at, SUB), :]
                    if cut:
                        keep = keep_ref[i * STEP + k]
                        s = [keep * v for v in s]
                    for n in range(modes):
                        s[n] = d[n] * s[n] + x
                    if emit is not None:
                        emit(at, x, s)
                return tuple(s)

            out = lax.fori_loop(
                0,
                span // STEP,
                run,
                tuple(s_ref[pl.ds(n * q8 + h, SUB), :] for n in range(modes)),
            )
            for n in range(modes):
                s_ref[pl.ds(n * q8 + h, SUB), :] = out[n]

    hit = opens(docs_ref, begin, span)

    @pl.when(hit)
    def _():
        mark(docs_ref, begin, span, keep_ref)
        sweep(True)

    @pl.when(jnp.logical_not(hit))
    def _():
        sweep(False)


def end_state_kernel(
    modes, q, q8, length, docs_ref, gate_ref, sig_ref, rates_ref, end_ref, x_ref, decay_ref,
    s_ref, keep_ref,
):
    step = pl.program_id(0)
    rows = gate_ref.shape[0]

    @pl.when(step == 0)
    def _():
        s_ref[...] = jnp.zeros_like(s_ref)
        fold(decay_ref, rates_ref, q, q8, lambda a: jnp.exp(-a))

    def tile(i, _):
        t0 = pl.multiple_of(i * 16, 16)
        for j in range(q):
            cols = pl.ds(j * LANES, LANES)
            x = gate_ref[pl.ds(t0, 16), cols].astype(jnp.float32) * sig_ref[
                pl.ds(t0, 16), cols
            ].astype(jnp.float32)
            x_ref[pl.ds(t0 * q8 + j, 16, stride=q8), :] = x
        return 0

    lax.fori_loop(0, rows // 16, tile, 0)

    begin = lax.axis_index("ctx") * length
    span = min(SPAN, rows)
    last = at = -begin
    for j in range(docs_ref.shape[0]):
        last = jnp.where(at < length, at, last)
        at = at + docs_ref[j]

    def piece(p, _):
        first = step * rows + p * span

        @pl.when(first + span > last)
        def _():
            recur(
                modes, q8, span, p * span, begin + first, docs_ref, keep_ref, decay_ref, s_ref,
                x_ref, lambda h: None,
            )

        return 0

    lax.fori_loop(0, rows // span, piece, 0)

    @pl.when(step == pl.num_programs(0) - 1)
    def _():
        end_ref[...] = s_ref[...].astype(end_ref.dtype)


def exchange_kernel(
    n, length, plan, q, q8, docs_ref, end_ref, rates_ref, out_ref, rate_ref, send_buf, slots,
    send_sem, recv_sem,
):
    me = lax.axis_index("ctx")
    offsets = sorted({off for stage in plan for off, _ in stage})
    barrier = pltpu.get_barrier_semaphore()
    for off in offsets:

        @pl.when(me >= off)
        def _():
            pl.semaphore_signal(
                barrier, inc=1, device_id={"ctx": me - off}, device_id_type=pl.DeviceIdType.MESH
            )

    peers = sum((me + off < n).astype(jnp.int32) for off in offsets)

    @pl.when(me + 1 < n)
    def _():
        pl.semaphore_wait(barrier, peers)

    def copy(k, stage, off):
        src = end_ref if stage == 0 else send_buf.at[stage - 1]
        return pltpu.make_async_remote_copy(
            src_ref=src,
            dst_ref=slots.at[k],
            send_sem=send_sem.at[k],
            recv_sem=recv_sem.at[k],
            device_id={"ctx": jnp.minimum(me + off, n - 1)},
            device_id_type=pl.DeviceIdType.MESH,
        )

    fold(rate_ref, rates_ref, q, q8, lambda a: a)
    start = head = jnp.int32(0)
    for j in range(docs_ref.shape[0]):
        head = jnp.where(start <= me * length, jnp.maximum(head, start), head)
        start = start + docs_ref[j]
    out_ref[...] = jnp.zeros_like(out_ref)
    k0 = 0
    for stage, hops in enumerate(plan):
        if stage:
            send_buf[stage - 1] = out_ref[...].astype(send_buf.dtype)
        for k, (off, gap) in enumerate(hops, k0):

            @pl.when(me + off < n)
            def _():
                copy(k, stage, off).start()

        for k, (off, gap) in enumerate(hops, k0):

            @pl.when(me >= off)
            def _():
                live = jnp.where(head < (me - gap) * length, 1.0, 0.0).astype(jnp.float32)
                weight = jnp.exp(rate_ref[...] * (-float(length * gap))) * live
                copy(k, stage, off).wait_recv()
                out_ref[...] += weight * slots[k].astype(jnp.float32)

        k0 += len(hops)
    k = 0
    for stage, hops in enumerate(plan):
        for off, gap in hops:

            @pl.when(me + off < n)
            def _():
                copy(k, stage, off).wait_send()

            k += 1


def conv_kernel(
    modes, q, q8, length, docs_ref, go_ref, x_ref, decay_ref, res_ref, gain_ref, carried_ref,
    w_ref, hidden_ref, near_ref, weight_ref, skip_ref, y_ref, s_ref, keep_ref, w_sem,
):
    step = pl.program_id(0)
    rows = go_ref.shape[0]
    fetch = pltpu.make_async_copy(w_ref, near_ref, w_sem)
    pl.when(step == 0)(fetch.start)

    @pl.when(step == 0)
    def _():
        s_ref[...] = carried_ref[...]
        fold(weight_ref, res_ref, q, q8, lambda a: a)
        fold(skip_ref, gain_ref, q, q8, lambda a: a)

    def emitter(h):
        r = [weight_ref[pl.ds(n * q8 + h, SUB), :] for n in range(modes)]
        skip = skip_ref[pl.ds(h, SUB), :]

        def emit(at, x, s):
            parts = [skip * x, None, None, None]
            for n in range(modes):
                term = r[n] * s[n]
                p = parts[n % 4]
                parts[n % 4] = term if p is None else p + term
            y_ref[pl.ds(at, SUB), :] = (parts[0] + parts[1]) + (parts[2] + parts[3])

        return emit

    span = min(SPAN, rows)
    begin = lax.axis_index("ctx") * length + step * rows

    def piece(p, _):
        recur(
            modes, q8, span, p * span, begin + p * span, docs_ref, keep_ref, decay_ref, s_ref,
            x_ref, emitter,
        )
        return 0

    lax.fori_loop(0, rows // span, piece, 0)

    def tile(i, _):
        t0 = pl.multiple_of(i * 16, 16)
        for j in range(q):
            cols = pl.ds(j * LANES, LANES)
            y = y_ref[pl.ds(t0 * q8 + j, 16, stride=q8), :]
            g = go_ref[pl.ds(t0, 16), cols].astype(jnp.float32)
            hidden_ref[pl.ds(t0, 16), cols] = (g * y).astype(hidden_ref.dtype)
        return 0

    lax.fori_loop(0, rows // 16, tile, 0)
    pl.when(step == pl.num_programs(0) - 1)(fetch.wait)


def project_kernel(
    hidden_ref, w_ref, out_ref, part_ref, own_buf, send_buf, recv_buf, send_sem, recv_sem
):
    tiles = own_buf.shape[0]
    half = own_buf.shape[1]
    tile = own_buf.shape[2]
    core = lax.axis_index("tp")
    barrier = pltpu.get_barrier_semaphore()
    pl.semaphore_signal(
        barrier, inc=1, device_id={"tp": 1 - core}, device_id_type=pl.DeviceIdType.MESH
    )
    pl.semaphore_wait(barrier, 1)

    def copy(k):
        return pltpu.make_async_remote_copy(
            src_ref=send_buf.at[k],
            dst_ref=recv_buf.at[k],
            send_sem=send_sem.at[k],
            recv_sem=recv_sem.at[k],
            device_id={"tp": 1 - core},
            device_id_type=pl.DeviceIdType.MESH,
        )

    def finish(k):
        copy(k).wait_recv()
        out_ref[:, pl.ds(pl.multiple_of(k * tile, tile), tile)] = (
            own_buf[k].astype(jnp.float32) + recv_buf[k].astype(jnp.float32)
        ).astype(out_ref.dtype)

    def step(j, _):
        cols = pl.ds(pl.multiple_of(j * tile, tile), tile)
        part_ref[...] = jnp.dot(
            hidden_ref[...], w_ref[:, cols], preferred_element_type=jnp.float32
        ).astype(part_ref.dtype)
        send_buf[j] = part_ref[pl.ds(pl.multiple_of((1 - core) * half, half), half), :]
        copy(j).start()
        own_buf[j] = part_ref[pl.ds(pl.multiple_of(core * half, half), half), :]

        @pl.when(j > 0)
        def _():
            finish(j - 1)

        return 0

    lax.fori_loop(0, tiles, step, 0)
    finish(tiles - 1)

    def drain(k, _):
        copy(k).wait_send()
        return 0

    lax.fori_loop(0, tiles, drain, 0)


def scan_plan(n, reach):
    plan = [[(off, off - 1) for off in range(1, min(4, n - 1) + 1)]]
    unit = 4
    while unit < n:
        plan.append([(off, off) for off in (unit, 2 * unit, 3 * unit) if off < min(n, reach)])
        unit *= 4
    return plan


def make(n, tp):
    def per_device(gate_out, gate_in, signal, decay_rates, residues, skip_gain, out_proj, doc_lengths):
        length, channels = signal.shape
        modes = decay_rates.shape[0]
        width = out_proj.shape[1]
        q = channels // LANES
        q8 = -(-q // SUB) * SUB
        chunk = min(CHUNK, length)
        flat = (modes * q8, LANES)
        params = pltpu.CompilerParams(vmem_limit_bytes=ROOM)
        smem = pl.BlockSpec(memory_space=pltpu.SMEM)
        vmem = pl.BlockSpec(memory_space=pltpu.VMEM)
        rows = pl.BlockSpec((chunk, channels), lambda i: (i, 0))
        folded = pl.BlockSpec((chunk * q8, LANES), lambda i: (i, 0))
        table = pl.BlockSpec((modes, channels), lambda i: (0, 0))
        state = pl.BlockSpec(flat, lambda i: (0, 0))
        plan = scan_plan(n, -(-(5 * n * length // 8) // length))
        hops = sum(len(stage) for stage in plan)
        flags = [pltpu.SMEM((SPAN,), jnp.float32)]
        end, feed, decay = pl.pallas_call(
            functools.partial(end_state_kernel, modes, q, q8, length),
            grid=(length // chunk,),
            out_shape=[
                jax.ShapeDtypeStruct(flat, jnp.bfloat16),
                jax.ShapeDtypeStruct((length * q8, LANES), jnp.float32),
                jax.ShapeDtypeStruct(flat, jnp.float32),
            ],
            in_specs=[smem, rows, rows, table],
            out_specs=[state, folded, state],
            scratch_shapes=[pltpu.VMEM(flat, jnp.float32)] + flags,
            compiler_params=params,
            name="end_state",
        )(doc_lengths, gate_in, signal, decay_rates)

        carried = pl.pallas_call(
            functools.partial(exchange_kernel, n, length, plan, q, q8),
            out_shape=jax.ShapeDtypeStruct(flat, jnp.float32),
            in_specs=[smem, vmem, vmem],
            out_specs=vmem,
            scratch_shapes=[
                pltpu.VMEM(flat, jnp.float32),
                pltpu.VMEM((max(len(plan) - 1, 1),) + flat, jnp.bfloat16),
                pltpu.VMEM((hops,) + flat, jnp.bfloat16),
                pltpu.SemaphoreType.DMA((hops,)),
                pltpu.SemaphoreType.DMA((hops,)),
            ],
            compiler_params=pltpu.CompilerParams(
                collective_id=0, has_side_effects=True, vmem_limit_bytes=ROOM
            ),
            name="state_exchange",
        )(doc_lengths, end, decay_rates)

        hidden, near = pl.pallas_call(
            functools.partial(conv_kernel, modes, q, q8, length),
            grid=(length // chunk,),
            out_shape=[
                pltpu.VMEM((length, channels), jnp.bfloat16),
                pltpu.VMEM(out_proj.shape, out_proj.dtype),
            ],
            in_specs=[smem, rows, folded, state, table,
                      pl.BlockSpec((1, channels), lambda i: (0, 0)), state,
                      pl.BlockSpec(memory_space=pltpu.HBM)],
            out_specs=[rows, pl.BlockSpec(memory_space=pl.ANY)],
            scratch_shapes=[
                pltpu.VMEM(flat, jnp.float32),
                pltpu.VMEM((q8, LANES), jnp.float32),
                pltpu.VMEM((chunk * q8, LANES), jnp.float32),
                pltpu.VMEM(flat, jnp.float32),
            ] + flags + [pltpu.SemaphoreType.DMA],
            compiler_params=pltpu.CompilerParams(vmem_limit_bytes=ROOM_CONV),
            name="conv",
        )(doc_lengths, gate_out, feed, decay, residues, skip_gain.reshape(1, channels), carried,
          out_proj)

        if tp != 2:
            part = jnp.dot(hidden, near, preferred_element_type=jnp.float32)
            return lax.psum_scatter(
                part.astype(jnp.bfloat16), "tp", scatter_dimension=0, tiled=True
            )
        half = length // 2
        tile = min(TILE, width)
        tiles = width // tile
        return pl.pallas_call(
            project_kernel,
            out_shape=jax.ShapeDtypeStruct((half, width), jnp.bfloat16),
            in_specs=[vmem, vmem],
            out_specs=vmem,
            scratch_shapes=[pltpu.VMEM((length, tile), jnp.bfloat16)]
            + [pltpu.VMEM((tiles, half, tile), jnp.bfloat16) for _ in range(3)]
            + [pltpu.SemaphoreType.DMA((tiles,)), pltpu.SemaphoreType.DMA((tiles,))],
            compiler_params=pltpu.CompilerParams(
                collective_id=1, has_side_effects=True, vmem_limit_bytes=ROOM_OUT
            ),
            name="project",
        )(hidden, near)

    return per_device


def solution(mesh):
    return jax.shard_map(
        make(mesh.shape["ctx"], mesh.shape["tp"]),
        mesh=mesh,
        in_specs=(
            P("ctx", "tp"),
            P("ctx", "tp"),
            P("ctx", "tp"),
            P(None, "tp"),
            P(None, "tp"),
            P("tp"),
            P("tp", None),
            P(),
        ),
        out_specs=P(("ctx", "tp"), None),
        check_vma=False,
    )
```
